32 devices in a mesh: ty: 2 (over x), tx: 16 (over z, y, core).
Axes of the slice: x: 2, y: 2, z: 4, core: 2. Of those that a mesh axis runs over, the one named last changes fastest.
Arguments:
- frame_zero: bfloat16 [32, 2048, 128], P('ty', 'tx'), may hold values from -6 to 6
- frame_one: bfloat16 [32, 2048, 128], P('ty', 'tx'), may hold values from -6 to 6
- offset_whole: int32 [2, 2, 32, 2048], P(None, None, 'ty', 'tx'), may hold values from -4 to 3
- offset_frac: float32 [2, 2, 32, 2048], P(None, None, 'ty', 'tx'), may hold values from 0 to 1
- list_tile: int32 [2, 2, 2, 16], P(None, None, 'ty', 'tx'), may hold values from 0 to 31, as said below
- list_pixel: int32 [2, 2, 2, 128], P(None, None, 'ty', 'tx'), may hold values from 0 to 7
- list_weight: bfloat16 [2, 2, 2, 128], P(None, None, 'ty', 'tx'), may hold values from 0.29882812 to 1
- conv_weight: bfloat16 [9, 256, 128], replicated, may hold values from -0.125 to 0.125
- conv_bias: float32 [128], replicated, may hold values from -3 to 3
- mix_weight: bfloat16 [128, 128], replicated, may hold values from -0.5 to 0.5
- mix_bias: float32 [128], replicated, may hold values from -3 to 3
- out_weight: bfloat16 [128, 2], replicated, may hold values from -0.5 to 0.5
- out_bias: float32 [2], replicated, may hold values from -3 to 3
Outputs:
- flow: float32 [2, 2, 32, 2048], P(None, None, 'ty', 'tx')
The draws below stay inside these ranges and needn't reach their ends.
Inputs may be any that keep to these rules, and one draw needn't show every extreme that they name: `list_tile`: for each direction and entry, every tile is named as a source by exactly one destination tile.
All inputs are finite; a program needn't handle non-finite values.
Results may differ from the reference program's by a relative error of at most 0.0021.
Values may be sent and summed in bfloat16 or wider, within the bound.
A program may use at most 64 MiB of HBM per device.

```python
import jax
import jax.numpy as jnp
from jax import lax

FEAT = 128
POOL = 16
MARGIN = 4
ENTRIES = 2
NY = 32
NX = 2048
CELL_ROWS = 1
CELL_COLS = 8
COARSE_ROWS = 2
COARSE_COLS = 128
N_TY = 2
N_TX = 16


def draw_list_tile(key, part):
    key = jax.random.fold_in(key, 11)
    keys = jax.random.split(key, 2 * ENTRIES)
    orders = [jax.random.permutation(keys[index], N_TY * N_TX) for index in range(2 * ENTRIES)]
    return jnp.stack(orders).reshape(2, ENTRIES, N_TY, N_TX).astype(jnp.int32)


def plant(entries, stream_key, least, largest):
    longest = entries.shape.index(max(entries.shape))
    spots = []
    for shift in (0, 1):
        where = [jax.random.randint(jax.random.fold_in(stream_key, axis), (), 0, length) for axis, length in enumerate(entries.shape)]
        where[longest] = (where[longest] + shift) % entries.shape[longest]
        spots.append(tuple(where))
    return entries.at[spots[0]].set(least).at[spots[1]].set(largest)


def steps_of(key, shape, pieces, low, top_value):
    level, own = 1.0, jax.random.fold_in(key, 6)
    for axis_at, parts in pieces:
        steps = jnp.exp(jax.random.uniform(jax.random.fold_in(own, axis_at), (parts,), jnp.float32, low / len(pieces), top_value / len(pieces)))
        level = level * jnp.repeat(steps, shape[axis_at] // parts).reshape([-1 if axis == axis_at else 1 for axis in range(len(shape))])
    return level


def centred(rng, dims, width, most, cuts=(), kind=jnp.bfloat16):
    loudness = steps_of(rng, dims, cuts, -0.22, 0.18) if cuts else 1.0
    values = jax.random.normal(rng, dims, jnp.float32) * width * loudness
    return jnp.minimum(jnp.maximum(values, -most), most).astype(kind)


def setup_inputs(seed: int = 0) -> dict:
    streams_of = jax.random.split(jax.random.key(seed), 14)
    return {
        "frame_zero": centred(streams_of[0], (NY, NX, FEAT), 1.0, 6.0, ((0, 2), (1, 16))),
        "frame_one": centred(streams_of[1], (NY, NX, FEAT), 1.0, 6.0, ((0, 2), (1, 16))),
        "offset_whole": plant(jax.random.randint(streams_of[2], (2, 2, NY, NX), 0 - MARGIN, MARGIN), jax.random.fold_in(streams_of[2], 1), 0 - MARGIN, MARGIN - 1).astype(jnp.int32),
        "offset_frac": jnp.clip(1.0 * jax.random.uniform(streams_of[3], (2, 2, NY, NX), jnp.float32) ** steps_of(streams_of[3], (2, 2, NY, NX), ((2, 2), (3, 16)), -0.2, 0.2), 0.0, 1.0),
        "list_tile": draw_list_tile(jax.random.fold_in(streams_of[13], 71), 0),
        "list_pixel": plant(jax.random.randint(streams_of[5], (2, ENTRIES, COARSE_ROWS, COARSE_COLS), 0, CELL_ROWS * CELL_COLS), jax.random.fold_in(streams_of[5], 1), 0, (CELL_ROWS * CELL_COLS) - 1).astype(jnp.int32),
        "list_weight": jnp.clip(0.29882812 + 0.7011719 * jax.random.uniform(streams_of[6], (2, ENTRIES, COARSE_ROWS, COARSE_COLS), jnp.float32) ** steps_of(streams_of[6], (2, ENTRIES, COARSE_ROWS, COARSE_COLS), ((2, 2), (3, 16)), -0.2, 0.2), 0.29882812, 1.0).astype(jnp.bfloat16),
        "conv_weight": centred(streams_of[7], (9, 2 * FEAT, FEAT), (18 * FEAT) ** -0.5, 0.125),
        "conv_bias": centred(streams_of[8], (FEAT,), 0.5, 3.0, (), jnp.float32),
        "mix_weight": centred(streams_of[9], (FEAT, FEAT), FEAT ** -0.5, 0.5),
        "mix_bias": centred(streams_of[10], (FEAT,), 0.5, 3.0, (), jnp.float32),
        "out_weight": centred(streams_of[11], (FEAT, 2), FEAT ** -0.5, 0.5),
        "out_bias": centred(streams_of[12], (2,), 1.0, 3.0, (), jnp.float32),
    }


def estimate(padded, conv_weight, conv_bias, mix_weight, mix_bias, out_weight, out_bias):
    tile_height = padded.shape[0] - 2
    tile_width = padded.shape[1] - 2
    summed = jnp.zeros((tile_height, tile_width, conv_weight.shape[2]), jnp.float32)
    for kernel_tap in range(9):
        shift_down = kernel_tap // 3
        shift_right = kernel_tap % 3
        summed = summed + jnp.dot(padded[shift_down:shift_down + tile_height, shift_right:shift_right + tile_width], conv_weight[kernel_tap], preferred_element_type=jnp.float32)
    hidden = jax.nn.relu(summed + conv_bias).astype(jnp.bfloat16)
    mixed_units = jax.nn.relu(jnp.dot(hidden, mix_weight, preferred_element_type=jnp.float32) + mix_bias).astype(jnp.bfloat16)
    return jnp.dot(mixed_units, out_weight, preferred_element_type=jnp.float32) + out_bias


def pool_cells(frames):
    count, row_total, col_total, channels = frames.shape
    blocks = frames.astype(jnp.float32).reshape(count, row_total // POOL, POOL, col_total // POOL, POOL, channels)
    return (jnp.sum(blocks, axis=(2, 4)) / POOL).astype(jnp.bfloat16)


def reference(frame_zero, frame_one, offset_whole, offset_frac, list_tile, list_pixel, list_weight, conv_weight, conv_bias, mix_weight, mix_bias, out_weight, out_bias):
    frames = jnp.stack([frame_zero, frame_one])
    coarse = pool_cells(frames)
    tile_rows = jnp.arange(COARSE_ROWS) // CELL_ROWS
    tile_cols = jnp.arange(COARSE_COLS) // CELL_COLS
    warped_cells = []
    for direction in range(2):
        source = coarse[1 - direction]
        summed = jnp.zeros((COARSE_ROWS, COARSE_COLS, FEAT), jnp.float32)
        for member in range(ENTRIES):
            source_tile = list_tile[direction, member][tile_rows][:, tile_cols]
            source_pixel = list_pixel[direction, member]
            source_row = (source_tile // N_TX) * CELL_ROWS + source_pixel // CELL_COLS
            source_col = (source_tile % N_TX) * CELL_COLS + source_pixel % CELL_COLS
            weight = list_weight[direction, member].astype(jnp.float32)
            summed = summed + weight[:, :, None] * source[source_row, source_col].astype(jnp.float32)
        warped_cells.append(summed.astype(jnp.bfloat16))
    coarse_cat = jnp.concatenate([coarse, jnp.stack(warped_cells)], axis=-1)
    coarse_flow = jnp.stack([estimate(jnp.pad(coarse_cat[direction], ((1, 1), (1, 1), (0, 0))), conv_weight, conv_bias, mix_weight, mix_bias, out_weight, out_bias) for direction in range(2)])
    upsampled = jnp.repeat(jnp.repeat(coarse_flow, POOL, axis=1), POOL, axis=2)
    row_ids = jnp.arange(NY)[:, None]
    col_ids = jnp.arange(NX)[None, :]
    flow_fields = []
    for direction in range(2):
        source = jnp.pad(frames[1 - direction], ((MARGIN, MARGIN), (MARGIN, MARGIN), (0, 0)))
        shift_down = offset_whole[direction, 0]
        across = offset_whole[direction, 1]
        frac_down = offset_frac[direction, 0]
        frac_across = offset_frac[direction, 1]
        summed = jnp.zeros((NY, NX, FEAT), jnp.float32)
        for corner_row in range(2):
            weight_row = frac_down if corner_row == 1 else 1.0 - frac_down
            for corner_col in range(2):
                weight_col = frac_across if corner_col == 1 else 1.0 - frac_across
                weight = lax.optimization_barrier((weight_row * weight_col).astype(jnp.bfloat16)).astype(jnp.float32)
                picked = source[row_ids + shift_down + corner_row + MARGIN, col_ids + across + corner_col + MARGIN]
                summed = summed + weight[:, :, None] * picked.astype(jnp.float32)
        warped = summed.astype(jnp.bfloat16)
        fine_cat = jnp.concatenate([frames[direction], warped], axis=-1)
        fine_flow = estimate(jnp.pad(fine_cat, ((1, 1), (1, 1), (0, 0))), conv_weight, conv_bias, mix_weight, mix_bias, out_weight, out_bias)
        flow_fields.append(fine_flow + upsampled[direction])
    return jnp.stack(flow_fields).transpose(0, 3, 1, 2)
```

```python
import functools

import jax
import jax.numpy as jnp
from jax import lax
from jax.experimental import pallas as pl
from jax.experimental.pallas import tpu as pltpu
from jax.sharding import PartitionSpec as P

POOL = 16
MARGIN = 4
EDGE = 16
DIRS = [(-1, 0), (1, 0), (0, -1), (0, 1), (-1, -1), (-1, 1), (1, -1), (1, 1)]
MESH = pl.DeviceIdType.MESH
BF = jnp.bfloat16
F32 = jnp.float32


def part(step, center, size, margin):
    if step < 0:
        return pl.ds(center - margin, margin)
    if step > 0:
        return pl.ds(center + size, margin)
    return pl.ds(center, size)


def rim(step, start, size, margin):
    if step < 0:
        return pl.ds(start, margin)
    if step > 0:
        return pl.ds(start + size - margin, margin)
    return pl.ds(start, size)


def nt(a, b):
    return lax.dot_general(a, b, (((1,), (1,)), ((), ())), preferred_element_type=F32)


def kernel(
    n_ty, n_tx, height, width,
    f0, f1, whole, frac, index, weight, conv_w, conv_b, mix_w, mix_b, out_w, out_b,
    out,
    F, F4, Wp, X, G, CW, T,
    load_sem, halo_send, halo_recv, all_send, all_recv, rim_send, rim_recv, cell_send, cell_recv,
):
    n = n_ty * n_tx
    ty, tx = lax.axis_index("ty"), lax.axis_index("tx")
    me = ty * n_tx + tx
    frames = (f0, f1)
    cells = width // POOL

    def has(dy, dx):
        return (ty + dy >= 0) & (ty + dy < n_ty) & (tx + dx >= 0) & (tx + dx < n_tx)

    def at(dy, dx):
        return (lax.rem(ty + dy + n_ty, n_ty), lax.rem(tx + dx + n_tx, n_tx))

    loads = [
        pltpu.make_async_copy(
            frames[f], F.at[f, pl.ds(MARGIN, height), pl.ds(EDGE, width)], load_sem.at[f]
        )
        for f in range(2)
    ]
    for load in loads:
        load.start()

    barrier = pltpu.get_barrier_semaphore()

    def greet(k, _):
        other = lax.rem(me + k, n)
        pl.semaphore_signal(
            barrier, inc=1, device_id=(other // n_tx, lax.rem(other, n_tx)), device_id_type=MESH
        )
        return 0

    lax.fori_loop(1, n, greet, 0)

    for dy, dx in DIRS:
        @pl.when(jnp.logical_not(has(dy, dx)))
        def _():
            rows, cols = part(dy, MARGIN, height, MARGIN), part(dx, EDGE, width, EDGE)
            F[:, rows, cols, :] = jnp.zeros((2, rows.size, cols.size, F.shape[3]), BF)
            rows = part(dy, 1, height, 1)
            Wp[:, rows, cols, :] = jnp.zeros((2, rows.size, cols.size, F.shape[3]), BF)

    pl.semaphore_wait(barrier, n - 1)

    def halo(s, f):
        dy, dx = DIRS[s]
        return pltpu.make_async_remote_copy(
            src_ref=frames[f].at[rim(dy, 0, height, MARGIN), rim(dx, 0, width, EDGE)],
            dst_ref=F.at[f, part(-dy, MARGIN, height, MARGIN), part(-dx, EDGE, width, EDGE)],
            send_sem=halo_send.at[s, f],
            recv_sem=halo_recv.at[s, f],
            device_id=at(dy, dx),
            device_id_type=MESH,
        )

    for s, (dy, dx) in enumerate(DIRS):
        @pl.when(has(dy, dx))
        def _():
            for f in range(2):
                halo(s, f).start()

    for load in loads:
        load.wait()
    pooled = []
    for f in range(2):
        def add_row(r, total):
            return total + F[f, MARGIN + r, EDGE : EDGE + width, :].astype(F32)

        total = lax.fori_loop(0, height, add_row, jnp.zeros((width, F.shape[3]), F32))
        pooled.append(jnp.sum(total.reshape(cells, POOL, -1), axis=1) / POOL)
    G[me] = jnp.concatenate(pooled, axis=0).astype(BF)

    def push(k):
        other = lax.rem(me + k, n)
        return pltpu.make_async_remote_copy(
            src_ref=G.at[me],
            dst_ref=G.at[me],
            send_sem=all_send.at[k],
            recv_sem=all_recv.at[k],
            device_id=(other // n_tx, lax.rem(other, n_tx)),
            device_id_type=MESH,
        )

    def push_start(k, _):
        push(k).start()
        return 0

    lax.fori_loop(1, n, push_start, 0)

    lane = lax.broadcasted_iota(jnp.int32, (8, 128), 1)
    pair = lax.broadcasted_iota(jnp.int32, (8, 128), 0)
    lane_row = (lane // 8) % 8
    lane_col = lane % 8
    source_lane = (2 * pair + lane // 64) * 8 + lane_col

    def blocked(rows):
        got = jnp.zeros((8, 128), rows.dtype)
        for r in range(8):
            row = jnp.broadcast_to(rows[r : r + 1, :], (8, 128))
            picked = jnp.take_along_axis(row, source_lane, axis=1, mode="promise_in_bounds")
            got = jnp.where(lane_row == r, picked, got)
        return got

    for d in range(2):
        for band in range(2):
            rows = pl.ds(band * 8, 8)
            a, b = blocked(whole[d, 0, rows, :]), blocked(whole[d, 1, rows, :])
            u, v = blocked(frac[d, 0, rows, :]), blocked(frac[d, 1, rows, :])
            here = 2 * d + band
            T[here, 0] = (a + lane_row + MARGIN).astype(F32)
            T[here, 1] = (b + lane_col + MARGIN).astype(F32)
            for i, w in enumerate(((1.0 - u) * (1.0 - v), (1.0 - u) * v, u * (1.0 - v), u * v)):
                T[here, 2 + i] = w.astype(BF).astype(F32)

    for s, (dy, dx) in enumerate(DIRS):
        @pl.when(has(-dy, -dx))
        def _():
            for f in range(2):
                halo(s, f).wait_recv()

    def shift(i, _):
        for f in range(2):
            F4[f, i, 0 : width + EDGE, :] = F[f, i, :, :][EDGE - MARGIN : EDGE - MARGIN + width + EDGE]
        return 0

    lax.fori_loop(0, height + 2 * MARGIN, shift, 0)

    sub = lax.broadcasted_iota(jnp.int32, (16, 128), 0).astype(F32)

    def warp(q, _):
        for d in range(2):
            for band in range(2):
                here = 2 * d + band
                ry, cx, w00, w01, w10, w11 = (
                    jnp.broadcast_to(T[here, i, pl.ds(q, 1), :], (16, 128)) for i in range(6)
                )
                first, second = sub == cx, sub == cx + 1.0
                upper = jnp.where(first, w00, jnp.where(second, w01, 0.0))
                lower = jnp.where(first, w10, jnp.where(second, w11, 0.0))
                levels = [
                    jnp.where(ry == float(y), upper, jnp.where(ry == float(y - 1), lower, 0.0)).astype(BF)
                    for y in range(16)
                ]
                matrix = jnp.concatenate(levels, axis=0).T
                near = F4[1 - d, pl.ds(band * 8, 16), pl.ds(pl.multiple_of(q * 16, 16), 32), :]
                blocks = []
                for k in range(2):
                    window = near[:, 8 * k : 8 * k + 16].reshape(256, -1)
                    made = jnp.dot(matrix[64 * k : 64 * k + 64], window, preferred_element_type=F32)
                    blocks.append(made.reshape(8, 8, -1))
                Wp[d, pl.ds(1 + band * 8, 8), pl.ds(pl.multiple_of(EDGE + q * 16, 16), 16), :] = (
                    jnp.concatenate(blocks, axis=1).astype(BF)
                )
        return 0

    lax.fori_loop(0, width // 16, warp, 0)

    def border(s):
        dy, dx = DIRS[s]
        return pltpu.make_async_remote_copy(
            src_ref=Wp.at[:, rim(dy, 1, height, 1), rim(dx, EDGE, width, EDGE)],
            dst_ref=Wp.at[:, part(-dy, 1, height, 1), part(-dx, EDGE, width, EDGE)],
            send_sem=rim_send.at[s],
            recv_sem=rim_recv.at[s],
            device_id=at(dy, dx),
            device_id_type=MESH,
        )

    for s, (dy, dx) in enumerate(DIRS):
        @pl.when(has(dy, dx))
        def _():
            border(s).start()

    def push_wait(k, _):
        push(k).wait_recv()
        return 0

    lax.fori_loop(1, n, push_wait, 0)
    every = G[...].reshape(n * 2 * cells, -1)
    source = lax.broadcasted_iota(jnp.int32, (2 * cells, n * 2 * cells), 1)
    warped = jnp.zeros((2 * cells, F.shape[3]), F32)
    for e in range(2):
        chosen = jnp.where(source == index[:, e : e + 1], weight[:, e : e + 1], 0.0).astype(BF)
        warped = warped + jnp.dot(chosen, every, preferred_element_type=F32)
    CW[8] = warped.astype(BF)

    def cell_copy(s):
        dy, dx = DIRS[s]
        return pltpu.make_async_remote_copy(
            src_ref=CW.at[8],
            dst_ref=CW.at[s],
            send_sem=cell_send.at[s],
            recv_sem=cell_recv.at[s],
            device_id=at(dy, dx),
            device_id_type=MESH,
        )

    for s, (dy, dx) in enumerate(DIRS):
        @pl.when(has(dy, dx))
        def _():
            cell_copy(s).start()

        @pl.when(jnp.logical_not(has(-dy, -dx)))
        def _():
            CW[s] = jnp.zeros(CW.shape[1:], BF)

    for s, (dy, dx) in enumerate(DIRS):
        @pl.when(has(-dy, -dx))
        def _():
            border(s).wait_recv()
            cell_copy(s).wait_recv()

    def head(summed):
        hidden = jnp.maximum(summed + conv_b[...], 0.0).astype(BF)
        mixed = jnp.dot(hidden, mix_w[...], preferred_element_type=F32) + mix_b[...]
        return jnp.maximum(mixed, 0.0).astype(BF)

    summed = jnp.zeros((2 * cells, F.shape[3]), F32)
    for dy in (-1, 0, 1):
        own, other = {}, {}
        for dx in (-1, 0, 1):
            oy, ox = at(dy, dx)
            there = has(dy, dx)
            own[dx] = jnp.where(there, G[oy * n_tx + ox].astype(F32), 0.0)
            slot = 8 if dy == 0 and dx == 0 else DIRS.index((-dy, -dx))
            other[dx] = CW[slot].astype(F32)
        columns = []
        for dx in (-1, 0, 1):
            for block in (own, other):
                sides = []
                for d in range(2):
                    lo = d * cells
                    mid = block[0][lo : lo + cells]
                    if dx < 0:
                        mid = jnp.concatenate([block[-1][lo + cells - 1 : lo + cells], mid[: cells - 1]], axis=0)
                    if dx > 0:
                        mid = jnp.concatenate([mid[1:], block[1][lo : lo + 1]], axis=0)
                    sides.append(mid)
                columns.append(jnp.concatenate(sides, axis=0).astype(BF))
        summed = summed + jnp.dot(
            jnp.concatenate(columns, axis=1), conv_w[dy + 1], preferred_element_type=F32
        )
    coarse = head(summed).astype(F32)
    ups = []
    for d in range(2):
        mine = coarse[d * cells : (d + 1) * cells]
        spread = jnp.broadcast_to(mine[:, None, :], (cells, POOL, mine.shape[1])).reshape(width, -1)
        ups.append(nt(out_w[...], spread.astype(BF)) + out_b[...])

    group = 4
    feat = F.shape[3]
    for d in range(2):
        def shifted(i, _):
            rows = (F[d, MARGIN - 1 + i], Wp[d, i])
            for k in range(2):
                for dx in range(3):
                    X[i, :, (2 * dx + k) * feat : (2 * dx + k + 1) * feat] = rows[k][
                        EDGE - 1 + dx : EDGE - 1 + dx + width
                    ]
            return 0

        lax.fori_loop(0, height + 2, shifted, 0)

        def conv(g, _):
            summed = jnp.zeros((group * width, feat), F32)
            for dy in range(3):
                block = X[pl.ds(g * group + dy, group)].reshape(group * width, 6 * feat)
                summed = summed + jnp.dot(block, conv_w[dy], preferred_element_type=F32)
            flow = nt(out_w[...], head(summed)) + out_b[...]
            for j in range(group):
                part_flow = flow[:, j * width : (j + 1) * width] + ups[d]
                for k in range(2):
                    out[d, k, pl.ds(g * group + j, 1), :] = part_flow[k : k + 1]
            return 0

        lax.fori_loop(0, height // group, conv, 0)

    for s, (dy, dx) in enumerate(DIRS):
        @pl.when(has(dy, dx))
        def _():
            for f in range(2):
                halo(s, f).wait_send()
            border(s).wait_send()
            cell_copy(s).wait_send()

    def push_done(k, _):
        push(k).wait_send()
        return 0

    lax.fori_loop(1, n, push_done, 0)


def on_device(
    n_ty, n_tx, frame_zero, frame_one, offset_whole, offset_frac, list_tile, list_pixel, list_weight,
    conv_weight, conv_bias, mix_weight, mix_bias, out_weight, out_bias,
):
    height, width, feat = frame_zero.shape
    cells = width // POOL
    n = n_ty * n_tx
    other = jnp.array([1, 0], jnp.int32).reshape(2, 1, 1, 1)
    index = list_tile * (2 * cells) + other * cells + list_pixel
    index = index.reshape(2, 2, cells).transpose(0, 2, 1).reshape(2 * cells, 2)
    weight = list_weight.reshape(2, 2, cells).transpose(0, 2, 1).reshape(2 * cells, 2).astype(F32)
    out_w = jnp.pad(out_weight.T, ((0, 6), (0, 0)))
    out_b = jnp.pad(out_bias.reshape(2, 1), ((0, 6), (0, 0)))
    vmem = pl.BlockSpec(memory_space=pltpu.VMEM)
    hbm = pl.BlockSpec(memory_space=pl.ANY)
    dma = pltpu.SemaphoreType.DMA
    return pl.pallas_call(
        functools.partial(kernel, n_ty, n_tx, height, width),
        out_shape=jax.ShapeDtypeStruct(offset_frac.shape, F32),
        in_specs=[hbm, hbm] + [vmem] * 10,
        out_specs=vmem,
        scratch_shapes=[
            pltpu.VMEM((2, height + 2 * MARGIN, width + 2 * EDGE, feat), BF),
            pltpu.VMEM((2, height + 2 * MARGIN, width + 2 * EDGE, feat), BF),
            pltpu.VMEM((2, height + 2, width + 2 * EDGE, feat), BF),
            pltpu.VMEM((height + 2, width, 6 * feat), BF),
            pltpu.VMEM((n, 2 * cells, feat), BF),
            pltpu.VMEM((9, 2 * cells, feat), BF),
            pltpu.VMEM((4, 6, 8, 128), F32),
            dma((2,)), dma((8, 2)), dma((8, 2)), dma((n,)), dma((n,)),
            dma((8,)), dma((8,)), dma((8,)), dma((8,)),
        ],
        compiler_params=pltpu.CompilerParams(
            collective_id=0, has_side_effects=True, vmem_limit_bytes=40 * 2**20
        ),
    )(
        frame_zero, frame_one, offset_whole, offset_frac, index, weight,
        conv_weight.reshape(3, 6 * feat, feat), conv_bias.reshape(1, -1), mix_weight,
        mix_bias.reshape(1, -1), out_w, out_b,
    )


def solution(mesh):
    tiles = P(None, None, "ty", "tx")
    in_specs = (P("ty", "tx", None),) * 2 + (tiles,) * 5 + (P(),) * 6
    run = functools.partial(on_device, mesh.shape["ty"], mesh.shape["tx"])
    return jax.shard_map(run, mesh=mesh, in_specs=in_specs, out_specs=tiles, check_vma=False)
```

```python
import functools

import jax
import jax.numpy as jnp
from jax import lax
from jax.experimental import pallas as pl
from jax.experimental.pallas import tpu as pltpu
from jax.sharding import PartitionSpec as P

POOL = 16
MARGIN = 4
EDGE = 16
DIRS = [(-1, 0), (1, 0), (0, -1), (0, 1), (-1, -1), (-1, 1), (1, -1), (1, 1)]
MESH = pl.DeviceIdType.MESH
BF = jnp.bfloat16
F32 = jnp.float32


def part(step, center, size, margin):
    if step < 0:
        return pl.ds(center - margin, margin)
    if step > 0:
        return pl.ds(center + size, margin)
    return pl.ds(center, size)


def rim(step, start, size, margin):
    if step < 0:
        return pl.ds(start, margin)
    if step > 0:
        return pl.ds(start + size - margin, margin)
    return pl.ds(start, size)


def nt(a, b):
    return lax.dot_general(a, b, (((1,), (1,)), ((), ())), preferred_element_type=F32)


def kernel(
    n_ty, n_tx, height, width,
    f0, f1, whole_in, frac_in, tiles, pixel_in, weight_in, conv_in, conv_b_in, mix_in, mix_b_in, out_in, out_b,
    out,
    F, F4, Wp, X, G, CW, T, whole, frac, pixel, weight, W2, mix2, conv_b, mix_b, out_w,
    load_sem, halo_send, halo_recv, all_send, all_recv, rim_send, rim_recv, side_send, side_recv, cell_send, cell_recv,
):
    n = n_ty * n_tx
    ty, tx = lax.axis_index("ty"), lax.axis_index("tx")
    me = ty * n_tx + tx
    frames = (f0, f1)
    cells = width // POOL
    feat = F.shape[3]

    def has(dy, dx):
        return (ty + dy >= 0) & (ty + dy < n_ty) & (tx + dx >= 0) & (tx + dx < n_tx)

    def at(dy, dx):
        return (lax.rem(ty + dy + n_ty, n_ty), lax.rem(tx + dx + n_tx, n_tx))

    barrier = pltpu.get_barrier_semaphore()

    def greet(k, _):
        other = lax.rem(me + k, n)
        pl.semaphore_signal(
            barrier, inc=1, device_id=(other // n_tx, lax.rem(other, n_tx)), device_id_type=MESH
        )
        return 0

    lax.fori_loop(1, n, greet, 0)

    moves = [(frames[f], F.at[f, pl.ds(MARGIN, height), pl.ds(EDGE, width)]) for f in range(2)]
    moves += [(whole_in, whole), (frac_in, frac), (pixel_in, pixel), (weight_in, weight)]
    moves += [
        (conv_in, W2.at[pl.ds(0, 3), :, pl.ds(0, feat)]),
        (conv_in, W2.at[pl.ds(1, 3), :, pl.ds(feat, feat)]),
        (mix_in, mix2.at[pl.ds(0, feat), pl.ds(0, feat)]),
        (mix_in, mix2.at[pl.ds(feat, feat), pl.ds(feat, feat)]),
        (conv_b_in, conv_b), (mix_b_in, mix_b), (out_in, out_w),
    ]
    loads = [pltpu.make_async_copy(src, dst, load_sem.at[i]) for i, (src, dst) in enumerate(moves)]
    for load in loads:
        load.start()

    for dy, dx in DIRS:
        @pl.when(jnp.logical_not(has(dy, dx)))
        def _():
            rows, cols = part(dy, MARGIN, height, MARGIN), part(dx, EDGE, width, EDGE)
            F[:, rows, cols, :] = jnp.zeros((2, rows.size, cols.size, feat), BF)
            rows = part(dy, 1, height, 1)
            Wp[:, rows, cols, :] = jnp.zeros((2, rows.size, cols.size, feat), BF)

    pl.semaphore_wait(barrier, n - 1)

    def halo(s, f):
        dy, dx = DIRS[s]
        return pltpu.make_async_remote_copy(
            src_ref=frames[f].at[rim(dy, 0, height, MARGIN), rim(dx, 0, width, EDGE)],
            dst_ref=F.at[f, part(-dy, MARGIN, height, MARGIN), part(-dx, EDGE, width, EDGE)],
            send_sem=halo_send.at[s, f],
            recv_sem=halo_recv.at[s, f],
            device_id=at(dy, dx),
            device_id_type=MESH,
        )

    for s, (dy, dx) in enumerate(DIRS):
        @pl.when(has(dy, dx))
        def _():
            for f in range(2):
                halo(s, f).start()

    def halo_wait(sides):
        for s in sides:
            dy, dx = DIRS[s]

            @pl.when(has(-dy, -dx))
            def _():
                for f in range(2):
                    halo(s, f).wait_recv()

    for load in loads[:2]:
        load.wait()
    pooled = []
    for f in range(2):
        def add_row(r, total):
            return total + F[f, MARGIN + r, EDGE : EDGE + width, :].astype(F32)

        total = lax.fori_loop(0, height, add_row, jnp.zeros((width, feat), F32))
        pooled.append(jnp.sum(total.reshape(cells, POOL, -1), axis=1) / POOL)
    G[me] = jnp.concatenate(pooled, axis=0).astype(BF)

    def push(k):
        other = lax.rem(me + k, n)
        return pltpu.make_async_remote_copy(
            src_ref=G.at[me],
            dst_ref=G.at[me],
            send_sem=all_send.at[k],
            recv_sem=all_recv.at[k],
            device_id=(other // n_tx, lax.rem(other, n_tx)),
            device_id_type=MESH,
        )

    def push_start(k, _):
        push(k).start()
        return 0

    lax.fori_loop(1, n, push_start, 0)

    for load in loads[2:]:
        load.wait()
    lane = lax.broadcasted_iota(jnp.int32, (8, 128), 1)
    pair = lax.broadcasted_iota(jnp.int32, (8, 128), 0)
    lane_row = (lane // 8) % 8
    lane_col = lane % 8
    source_lane = (2 * pair + lane // 64) * 8 + lane_col

    def blocked(rows):
        got = jnp.zeros((8, 128), rows.dtype)
        for r in range(8):
            row = jnp.broadcast_to(rows[r : r + 1, :], (8, 128))
            picked = jnp.take_along_axis(row, source_lane, axis=1, mode="promise_in_bounds")
            got = jnp.where(lane_row == r, picked, got)
        return got

    for d in range(2):
        for band in range(2):
            rows = pl.ds(band * 8, 8)
            a, b = blocked(whole[d, 0, rows, :]), blocked(whole[d, 1, rows, :])
            u, v = blocked(frac[d, 0, rows, :]), blocked(frac[d, 1, rows, :])
            here = 2 * d + band
            T[here, 0] = (a + lane_row + MARGIN).astype(F32)
            T[here, 1] = (b + lane_col + MARGIN).astype(F32)
            for i, w in enumerate(((1.0 - u) * (1.0 - v), (1.0 - u) * v, u * (1.0 - v), u * v)):
                T[here, 2 + i] = w.astype(BF).astype(F32)

    W2[0, :, feat:] = jnp.zeros((6 * feat, feat), BF)
    W2[3, :, :feat] = jnp.zeros((6 * feat, feat), BF)
    mix2[:feat, feat:] = jnp.zeros((feat, feat), BF)
    mix2[feat:, :feat] = jnp.zeros((feat, feat), BF)
    flat = jnp.concatenate([out_w[...].astype(F32), jnp.zeros((6, feat), F32)], axis=0)
    lower = jnp.concatenate([jnp.zeros((2, feat), F32), flat[:6]], axis=0)
    out_two = jnp.concatenate([flat, lower], axis=1).astype(BF)
    out_one = flat.astype(BF)

    def shift(i):
        for f in range(2):
            F4[f, i, 0 : width + EDGE, :] = F[f, i, :, :][EDGE - MARGIN : EDGE - MARGIN + width + EDGE]

    def spread(k, i):
        for d in range(2):
            row = F[d, MARGIN - 1 + i] if k == 0 else Wp[d, i]
            for dx in range(3):
                X[d, i, :, (2 * dx + k) * feat : (2 * dx + k + 1) * feat] = row[
                    EDGE - 1 + dx : EDGE - 1 + dx + width
                ]

    def loop(count, start, step):
        def once(i, _):
            step(start + i)
            return 0

        lax.fori_loop(0, count, once, 0)

    sub = lax.broadcasted_iota(jnp.int32, (16, 128), 0).astype(F32)

    def warp_pair(band, d, q):
        here = 2 * d + band
        ry, cx, w00, w01, w10, w11 = (
            jnp.broadcast_to(T[here, i, pl.ds(q, 1), :], (16, 128)) for i in range(6)
        )
        first, second = sub == cx, sub == cx + 1.0
        upper = jnp.where(first, w00, jnp.where(second, w01, 0.0))
        lower = jnp.where(first, w10, jnp.where(second, w11, 0.0))
        levels = [
            jnp.where(ry == float(y), upper, jnp.where(ry == float(y - 1), lower, 0.0)).astype(BF)
            for y in range(16)
        ]
        matrix = jnp.concatenate(levels, axis=0).T
        near = F4[1 - d, pl.ds(band * 8, 16), pl.ds(pl.multiple_of(q * 16, 16), 32), :]
        blocks = []
        for k in range(2):
            window = near[:, 8 * k : 8 * k + 16].reshape(256, -1)
            made = jnp.dot(matrix[64 * k : 64 * k + 64], window, preferred_element_type=F32)
            blocks.append(made.reshape(8, 8, -1))
        Wp[d, pl.ds(1 + band * 8, 8), pl.ds(pl.multiple_of(EDGE + q * 16, 16), 16), :] = (
            jnp.concatenate(blocks, axis=1).astype(BF)
        )

    def warp(band):
        def two(i):
            for q in range(2):
                for d in range(2):
                    warp_pair(band, d, 2 * i + q)

        loop(width // 32, 0, two)

    def side(s, band, turn):
        dy, dx = DIRS[s]
        rows = pl.ds(1 + 8 * band, 8)
        return pltpu.make_async_remote_copy(
            src_ref=Wp.at[:, rows, rim(dx, EDGE, width, EDGE)],
            dst_ref=Wp.at[:, rows, part(-dx, EDGE, width, EDGE)],
            send_sem=side_send.at[s, turn],
            recv_sem=side_recv.at[s, turn],
            device_id=at(dy, dx),
            device_id_type=MESH,
        )

    def border(s):
        dy, dx = DIRS[s]
        return pltpu.make_async_remote_copy(
            src_ref=Wp.at[:, rim(dy, 1, height, 1), rim(dx, EDGE, width, EDGE)],
            dst_ref=Wp.at[:, part(-dy, 1, height, 1), part(-dx, EDGE, width, EDGE)],
            send_sem=rim_send.at[s],
            recv_sem=rim_recv.at[s],
            device_id=at(dy, dx),
            device_id_type=MESH,
        )

    def cell_copy(s):
        dy, dx = DIRS[s]
        return pltpu.make_async_remote_copy(
            src_ref=CW.at[8],
            dst_ref=CW.at[s],
            send_sem=cell_send.at[s],
            recv_sem=cell_recv.at[s],
            device_id=at(dy, dx),
            device_id_type=MESH,
        )

    def each(sides, sign, act):
        for s in sides:
            dy, dx = DIRS[s]

            @pl.when(has(sign * dy, sign * dx))
            def _():
                act(s)

    across = (2, 3)
    along = (0, 1, 4, 5, 6, 7)
    everywhere = range(8)

    def coarse_warp():
        def push_wait(k, _):
            push(k).wait_recv()
            return 0

        lax.fori_loop(1, n, push_wait, 0)
        every = G[...].reshape(n * 2 * cells, -1)
        source = lax.broadcasted_iota(jnp.int32, (2 * cells, n * 2 * cells), 1).astype(F32)
        small = lax.broadcasted_iota(jnp.int32, (cells, cells), 0) == lax.broadcasted_iota(
            jnp.int32, (cells, cells), 1
        )
        warped = jnp.zeros((2 * cells, feat), F32)
        for e in range(2):
            names, shares = [], []
            for d in range(2):
                base = tiles[d, 0, 0, e] * (2 * cells) + (1 - d) * cells
                row = (pixel[d, e] + base).astype(F32)
                names.append(jnp.sum(jnp.where(small, row, 0.0), axis=1, keepdims=True))
                row = weight[d, 0][e : e + 1].astype(F32)
                shares.append(jnp.sum(jnp.where(small, row, 0.0), axis=1, keepdims=True))
            names, shares = jnp.concatenate(names, axis=0), jnp.concatenate(shares, axis=0)
            chosen = jnp.where(source == names, shares, 0.0).astype(BF)
            warped = warped + jnp.dot(chosen, every, preferred_element_type=F32)
        CW[8] = warped.astype(BF)
        for s, (dy, dx) in enumerate(DIRS):
            @pl.when(jnp.logical_not(has(-dy, -dx)))
            def _():
                CW[s] = jnp.zeros(CW.shape[1:], BF)

        each(everywhere, 1, lambda s: cell_copy(s).start())

    def coarse_flow():
        each(everywhere, -1, lambda s: cell_copy(s).wait_recv())
        summed = jnp.zeros((2 * cells, feat), F32)
        for dy in (-1, 0, 1):
            own, other = {}, {}
            for dx in (-1, 0, 1):
                oy, ox = at(dy, dx)
                there = has(dy, dx)
                own[dx] = jnp.where(there, G[oy * n_tx + ox].astype(F32), 0.0)
                slot = 8 if dy == 0 and dx == 0 else DIRS.index((-dy, -dx))
                other[dx] = CW[slot].astype(F32)
            columns = []
            for dx in (-1, 0, 1):
                for block in (own, other):
                    sides = []
                    for d in range(2):
                        lo = d * cells
                        mid = block[0][lo : lo + cells]
                        if dx < 0:
                            mid = jnp.concatenate([block[-1][lo + cells - 1 : lo + cells], mid[: cells - 1]], axis=0)
                        if dx > 0:
                            mid = jnp.concatenate([mid[1:], block[1][lo : lo + 1]], axis=0)
                        sides.append(mid)
                    columns.append(jnp.concatenate(sides, axis=0).astype(BF))
            summed = summed + jnp.dot(
                jnp.concatenate(columns, axis=1), W2[dy + 1, :, :feat], preferred_element_type=F32
            )
        hidden = jnp.maximum(summed + conv_b[...], 0.0).astype(BF)
        mixed = jnp.dot(hidden, mix2[:feat, :feat], preferred_element_type=F32) + mix_b[...]
        coarse = jnp.maximum(mixed, 0.0)
        ups = []
        for d in range(2):
            mine = coarse[d * cells : (d + 1) * cells]
            wide = jnp.broadcast_to(mine[:, None, :], (cells, POOL, feat)).reshape(width, -1)
            ups.append(nt(out_one, wide.astype(BF)))
        return ups

    conv_b2 = jnp.concatenate([conv_b[...]] * 2, axis=1)
    mix_b2 = jnp.concatenate([mix_b[...]] * 2, axis=1)

    def conv(start, pairs):
        def one(d):
            lhs = jnp.concatenate(
                [
                    jnp.concatenate([X[d, start + 2 * p + s] for p in range(pairs)], axis=0)
                    for s in range(4)
                ],
                axis=1,
            )
            summed = jnp.dot(lhs, W2[...].reshape(4 * 6 * feat, 2 * feat), preferred_element_type=F32)
            hidden = jnp.maximum(summed + conv_b2, 0.0).astype(BF)
            mixed = jnp.dot(hidden, mix2[...], preferred_element_type=F32) + mix_b2
            flow = nt(out_two, jnp.maximum(mixed, 0.0).astype(BF))
            for p in range(pairs):
                for j in range(2):
                    for k in range(2):
                        out[d, k, pl.ds(start + 2 * p + j, 1), :] = (
                            flow[2 * j + k : 2 * j + k + 1, p * width : (p + 1) * width] + out_b[k]
                        )

        loop(2, 0, one)

    if n_ty == 2:
        one = ty
        two = 1 - ty
        halo_wait(across)
        loop(height + MARGIN, MARGIN * one, shift)
        loop(height + 1, one, functools.partial(spread, 0))
        warp(one)
        each(across, 1, lambda s: side(s, one, 0).start())
        coarse_warp()
        each(across, -1, lambda s: side(s, one, 0).wait_recv())
        loop(9, 9 * one, functools.partial(spread, 1))
        conv(10 * one, 3)
        halo_wait(along)
        loop(MARGIN, (height + MARGIN) * two, shift)
        spread(0, (height + 1) * two)
        warp(two)
        each(along, 1, lambda s: border(s).start())
        each(across, 1, lambda s: side(s, two, 1).start())
        ups = coarse_flow()
        each(across, -1, lambda s: side(s, two, 1).wait_recv())
        loop(8, 1 + 8 * two, functools.partial(spread, 1))
        conv(2 + 4 * two, 4)
        each(along, -1, lambda s: border(s).wait_recv())
        spread(1, (height + 1) * two)
        conv(14 * two, 1)
    else:
        one, two = 0, 1
        halo_wait(everywhere)
        loop(height + 2 * MARGIN, 0, shift)
        loop(height + 2, 0, functools.partial(spread, 0))
        warp(0)
        warp(1)
        each(along, 1, lambda s: border(s).start())
        each(across, 1, lambda s: side(s, 0, 0).start())
        each(across, 1, lambda s: side(s, 1, 1).start())
        coarse_warp()
        ups = coarse_flow()
        each(along, -1, lambda s: border(s).wait_recv())
        each(across, -1, lambda s: side(s, 0, 0).wait_recv())
        each(across, -1, lambda s: side(s, 1, 1).wait_recv())
        loop(height + 2, 0, functools.partial(spread, 1))
        conv(0, 4)
        conv(8, 4)

    for d in range(2):
        for k in range(2):
            out[d, k] = out[d, k] + (ups[d][k : k + 1] + out_b[k])

    for f in range(2):
        each(everywhere, 1, lambda s: halo(s, f).wait_send())
    each(along, 1, lambda s: border(s).wait_send())
    each(across, 1, lambda s: side(s, one, 0).wait_send())
    each(across, 1, lambda s: side(s, two, 1).wait_send())
    each(everywhere, 1, lambda s: cell_copy(s).wait_send())

    def push_done(k, _):
        push(k).wait_send()
        return 0

    lax.fori_loop(1, n, push_done, 0)


def on_device(
    n_ty, n_tx, frame_zero, frame_one, offset_whole, offset_frac, list_tile, list_pixel, list_weight,
    conv_weight, conv_bias, mix_weight, mix_bias, out_weight, out_bias,
):
    height, width, feat = frame_zero.shape
    cells = width // POOL
    n = n_ty * n_tx
    vmem = pl.BlockSpec(memory_space=pltpu.VMEM)
    smem = pl.BlockSpec(memory_space=pltpu.SMEM)
    hbm = pl.BlockSpec(memory_space=pl.ANY)
    dma = pltpu.SemaphoreType.DMA
    return pl.pallas_call(
        functools.partial(kernel, n_ty, n_tx, height, width),
        out_shape=jax.ShapeDtypeStruct(offset_frac.shape, F32),
        in_specs=[hbm] * 4 + [smem] + [hbm] * 7 + [smem],
        out_specs=vmem,
        scratch_shapes=[
            pltpu.VMEM((2, height + 2 * MARGIN, width + 2 * EDGE, feat), BF),
            pltpu.VMEM((2, height + 2 * MARGIN, width + EDGE, feat), BF),
            pltpu.VMEM((2, height + 2, width + 2 * EDGE, feat), BF),
            pltpu.VMEM((2, height + 2, width, 6 * feat), BF),
            pltpu.VMEM((n, 2 * cells, feat), BF),
            pltpu.VMEM((9, 2 * cells, feat), BF),
            pltpu.VMEM((4, 6, 8, 128), F32),
            pltpu.VMEM(offset_whole.shape, jnp.int32),
            pltpu.VMEM(offset_frac.shape, F32),
            pltpu.VMEM(list_pixel.shape, jnp.int32),
            pltpu.VMEM((2, 1, 2, cells), BF),
            pltpu.VMEM((4, 6 * feat, 2 * feat), BF),
            pltpu.VMEM((2 * feat, 2 * feat), BF),
            pltpu.VMEM((1, feat), F32),
            pltpu.VMEM((1, feat), F32),
            pltpu.VMEM((2, feat), BF),
            dma((13,)), dma((8, 2)), dma((8, 2)), dma((n,)), dma((n,)),
            dma((8,)), dma((8,)), dma((8, 2)), dma((8, 2)), dma((8,)), dma((8,)),
        ],
        compiler_params=pltpu.CompilerParams(
            collective_id=0, has_side_effects=True, vmem_limit_bytes=60 * 2**20
        ),
    )(
        frame_zero, frame_one, offset_whole, offset_frac, list_tile.transpose(0, 2, 3, 1), list_pixel,
        list_weight.transpose(0, 2, 1, 3), conv_weight.reshape(3, 6 * feat, feat), conv_bias.reshape(1, -1), mix_weight,
        mix_bias.reshape(1, -1), out_weight.T, out_bias,
    )


def solution(mesh):
    tiles = P(None, None, "ty", "tx")
    in_specs = (P("ty", "tx", None),) * 2 + (tiles,) * 5 + (P(),) * 6
    run = functools.partial(on_device, mesh.shape["ty"], mesh.shape["tx"])
    return jax.shard_map(run, mesh=mesh, in_specs=in_specs, out_specs=tiles, check_vma=False)
```

```python
import functools

import jax
import jax.numpy as jnp
from jax import lax
from jax.experimental import pallas as pl
from jax.experimental.pallas import tpu as pltpu
from jax.sharding import PartitionSpec as P

POOL = 16
MARGIN = 4
EDGE = 16
DIRS = [(-1, 0), (1, 0), (0, -1), (0, 1), (-1, -1), (-1, 1), (1, -1), (1, 1)]
MESH = pl.DeviceIdType.MESH
BF = jnp.bfloat16
F32 = jnp.float32


def part(step, center, size, margin):
    if step < 0:
        return pl.ds(center - margin, margin)
    if step > 0:
        return pl.ds(center + size, margin)
    return pl.ds(center, size)


def rim(step, start, size, margin):
    if step < 0:
        return pl.ds(start, margin)
    if step > 0:
        return pl.ds(start + size - margin, margin)
    return pl.ds(start, size)


def nt(a, b):
    return lax.dot_general(a, b, (((1,), (1,)), ((), ())), preferred_element_type=F32)


def kernel(
    n_ty, n_tx, height, width,
    f0, f1, whole_in, frac_in, tiles, pixel_in, weight_in, conv_in, conv_b_in, mix_in, mix_b_in, out_in, out_b,
    out,
    F, F4, Wp, X, G, CW, T, LB, PO, PI, CI, SO, SI, SC, whole, frac, pixel, weight, W2, mix2, conv_b, mix_b, out_w,
    load_sem, halo_send, halo_recv, all_send, all_recv, rim_send, rim_recv, side_send, side_recv, list_send, list_recv,
):
    n = n_ty * n_tx
    ty, tx = lax.axis_index("ty"), lax.axis_index("tx")
    tx_bits, ty_bits = n_tx.bit_length() - 1, n_ty.bit_length() - 1
    assert n_tx == 1 << tx_bits and n_ty == 1 << ty_bits
    steps = [(1, b) for b in range(tx_bits - 1, 0, -1)] + [(0, b) for b in range(ty_bits - 1, -1, -1)]
    steps += [(1, 0)] if tx_bits else []

    def slot_of(place):
        return sum(lax.rem(place[which] // (1 << b), 2) * (1 << j) for j, (which, b) in enumerate(steps))

    me = slot_of((ty, tx))
    frames = (f0, f1)
    cells = width // POOL
    feat = F.shape[3]

    def has(dy, dx):
        return (ty + dy >= 0) & (ty + dy < n_ty) & (tx + dx >= 0) & (tx + dx < n_tx)

    def at(dy, dx):
        return (lax.rem(ty + dy + n_ty, n_ty), lax.rem(tx + dx + n_tx, n_tx))

    barrier = pltpu.get_barrier_semaphore()

    def mate(step):
        which, b = step
        place = [ty, tx]
        place[which] = place[which] + (1 << b) * (1 - 2 * lax.rem(place[which] // (1 << b), 2))
        return tuple(place)

    def greet(there):
        pl.semaphore_signal(barrier, inc=1, device_id=there, device_id_type=MESH)

    for dy, dx in DIRS:
        @pl.when(has(dy, dx))
        def _():
            greet(at(dy, dx))

    far = [step for step in steps if step[1] > 0]
    for step in far:
        greet(mate(step))

    moves = [(frames[f], F.at[f, pl.ds(MARGIN, height), pl.ds(EDGE, width)]) for f in range(2)]
    moves += [(whole_in, whole), (frac_in, frac), (pixel_in, pixel), (weight_in, weight)]
    moves += [
        (conv_in, W2.at[pl.ds(0, 3), :, pl.ds(0, feat)]),
        (conv_in, W2.at[pl.ds(1, 3), :, pl.ds(feat, feat)]),
        (mix_in, mix2.at[pl.ds(0, feat), pl.ds(0, feat)]),
        (mix_in, mix2.at[pl.ds(feat, feat), pl.ds(feat, feat)]),
        (conv_b_in, conv_b), (mix_b_in, mix_b), (out_in, out_w),
    ]
    loads = [pltpu.make_async_copy(src, dst, load_sem.at[i]) for i, (src, dst) in enumerate(moves)]
    for load in loads:
        load.start()

    for dy, dx in DIRS:
        @pl.when(jnp.logical_not(has(dy, dx)))
        def _():
            rows, cols = part(dy, MARGIN, height, MARGIN), part(dx, EDGE, width, EDGE)
            F[:, rows, cols, :] = jnp.zeros((2, rows.size, cols.size, feat), BF)
            rows = part(dy, 1, height, 1)
            Wp[:, rows, cols, :] = jnp.zeros((2, rows.size, cols.size, feat), BF)

    for load in loads[4:6]:
        load.wait()
    LB[8] = jnp.zeros((8, 128), F32)
    for d in range(2):
        for e in range(2):
            tile = tiles[d, 0, 0, e]
            base = slot_of((tile // n_tx, lax.rem(tile, n_tx))) * (2 * cells) + (1 - d) * cells
            LB[8, 2 * d + e : 2 * d + e + 1, :cells] = (pixel[d, e] + base).astype(F32)
            LB[8, 4 + 2 * d + e : 5 + 2 * d + e, :cells] = weight[d, 0].astype(F32)[e : e + 1]
    for s, (dy, dx) in enumerate(DIRS):
        @pl.when(jnp.logical_not(has(-dy, -dx)))
        def _():
            LB[s] = jnp.zeros((8, 128), F32)

    for load in loads[:2]:
        load.wait()

    def pack(g, _):
        for f in range(2):
            rows = [MARGIN + 4 * g + i for i in range(4)]
            left = [F[f, row, EDGE : 2 * EDGE, :].astype(F32)[:MARGIN] for row in rows]
            right = [F[f, row, width : width + EDGE, :].astype(F32)[EDGE - MARGIN :] for row in rows]
            here = pl.ds(pl.multiple_of(16 * g, 16), 16)
            PO[0, f, here, :] = jnp.concatenate(left, axis=0).astype(BF)
            PO[1, f, here, :] = jnp.concatenate(right, axis=0).astype(BF)
        return 0

    lax.fori_loop(0, height // 4, pack, 0)

    peers = sum(jnp.where(has(dy, dx), 1, 0) for dy, dx in DIRS) + len(far)
    pl.semaphore_wait(barrier, peers)

    def halo(s):
        dy, dx = DIRS[s]
        hand = 0 if dx < 0 else 1
        if dx == 0:
            src = F.at[:, rim(dy, MARGIN, height, MARGIN), pl.ds(EDGE, width)]
            dst = F.at[:, part(-dy, MARGIN, height, MARGIN), pl.ds(EDGE, width)]
        elif dy == 0:
            src, dst = PO.at[hand], PI.at[hand]
        else:
            src, dst = PO.at[hand, :, pl.ds(0 if dy < 0 else 4 * height - 16, 16)], CI.at[s - 4]
        return pltpu.make_async_remote_copy(
            src_ref=src,
            dst_ref=dst,
            send_sem=halo_send.at[s],
            recv_sem=halo_recv.at[s],
            device_id=at(dy, dx),
            device_id_type=MESH,
        )

    def list_copy(s):
        return pltpu.make_async_remote_copy(
            src_ref=LB.at[8],
            dst_ref=LB.at[s],
            send_sem=list_send.at[s],
            recv_sem=list_recv.at[s],
            device_id=at(*DIRS[s]),
            device_id_type=MESH,
        )

    for s in (2, 3, 4, 5, 6, 7, 0, 1):
        @pl.when(has(*DIRS[s]))
        def _():
            halo(s).start()

    for s in range(8):
        @pl.when(has(*DIRS[s]))
        def _():
            list_copy(s).start()

    def unpack(tile, f, start, hand):
        tile = tile.astype(F32)
        rest = jnp.zeros((EDGE - MARGIN, feat), F32)
        for i in range(4):
            piece = tile[4 * i : 4 * i + 4]
            if hand == 0:
                F[f, start + i, EDGE + width :, :] = jnp.concatenate([piece, rest], axis=0).astype(BF)
            else:
                F[f, start + i, :EDGE, :] = jnp.concatenate([rest, piece], axis=0).astype(BF)

    def halo_wait(sides):
        for s in sides:
            dy, dx = DIRS[s]

            @pl.when(has(-dy, -dx))
            def _():
                halo(s).wait_recv()
                hand = 0 if dx < 0 else 1
                for f in range(2):
                    if dx != 0 and dy == 0:
                        def group(g, _):
                            tile = PI[hand, f, pl.ds(pl.multiple_of(16 * g, 16), 16), :]
                            unpack(tile, f, MARGIN + 4 * g, hand)
                            return 0

                        lax.fori_loop(0, height // 4, group, 0)
                    elif dx != 0:
                        unpack(CI[s - 4, f], f, MARGIN + height if dy < 0 else 0, hand)

    pooled = []
    for f in range(2):
        def add_row(r, total):
            return total + F[f, MARGIN + r, EDGE : EDGE + width, :].astype(F32)

        total = lax.fori_loop(0, height, add_row, jnp.zeros((width, feat), F32))
        pooled.append(jnp.sum(total.reshape(cells, POOL, -1), axis=1) / POOL)
    G[me] = jnp.concatenate(pooled, axis=0).astype(BF)

    def hand(j):
        span = 1 << j
        held = pl.ds(me - lax.rem(me, span), span)
        return pltpu.make_async_remote_copy(
            src_ref=G.at[held],
            dst_ref=G.at[held],
            send_sem=all_send.at[j],
            recv_sem=all_recv.at[j],
            device_id=mate(steps[j]),
            device_id_type=MESH,
        )

    def hand_on(j):
        if j > 0 and j <= len(steps):
            hand(j - 1).wait_recv()
        if j < len(steps):
            hand(j).start()

    hand_on(0)

    for load in loads[2:4] + loads[6:]:
        load.wait()
    lane = lax.broadcasted_iota(jnp.int32, (8, 128), 1)
    pair = lax.broadcasted_iota(jnp.int32, (8, 128), 0)
    lane_row = (lane // 8) % 8
    lane_col = lane % 8
    source_lane = (2 * pair + lane // 64) * 8 + lane_col

    def blocked(rows):
        got = jnp.zeros((8, 128), rows.dtype)
        for r in range(8):
            row = jnp.broadcast_to(rows[r : r + 1, :], (8, 128))
            picked = jnp.take_along_axis(row, source_lane, axis=1, mode="promise_in_bounds")
            got = jnp.where(lane_row == r, picked, got)
        return got

    for d in range(2):
        for band in range(2):
            rows = pl.ds(band * 8, 8)
            a, b = blocked(whole[d, 0, rows, :]), blocked(whole[d, 1, rows, :])
            u, v = blocked(frac[d, 0, rows, :]), blocked(frac[d, 1, rows, :])
            here = 2 * d + band
            T[here, 0] = (a + lane_row + MARGIN).astype(F32)
            T[here, 1] = (b + lane_col + MARGIN).astype(F32)
            for i, w in enumerate(((1.0 - u) * (1.0 - v), (1.0 - u) * v, u * (1.0 - v), u * v)):
                T[here, 2 + i] = w.astype(BF).astype(F32)

    W2[0, :, feat:] = jnp.zeros((6 * feat, feat), BF)
    W2[3, :, :feat] = jnp.zeros((6 * feat, feat), BF)
    mix2[:feat, feat:] = jnp.zeros((feat, feat), BF)
    mix2[feat:, :feat] = jnp.zeros((feat, feat), BF)
    flat = jnp.concatenate([out_w[...].astype(F32), jnp.zeros((6, feat), F32)], axis=0)
    lower = jnp.concatenate([jnp.zeros((2, feat), F32), flat[:6]], axis=0)
    out_two = jnp.concatenate([flat, lower], axis=1).astype(BF)
    out_one = flat.astype(BF)

    def shift(i):
        for f in range(2):
            F4[f, i, 0 : width + EDGE, :] = F[f, i, :, :][EDGE - MARGIN : EDGE - MARGIN + width + EDGE]

    def spread(k, i):
        for d in range(2):
            row = F[d, MARGIN - 1 + i] if k == 0 else Wp[d, i]
            for dx in range(3):
                X[d, i, :, (2 * dx + k) * feat : (2 * dx + k + 1) * feat] = row[
                    EDGE - 1 + dx : EDGE - 1 + dx + width
                ]

    def loop(count, start, step):
        def once(i, _):
            step(start + i)
            return 0

        lax.fori_loop(0, count, once, 0)

    sub = lax.broadcasted_iota(jnp.int32, (16, 128), 0).astype(F32)

    def warp_pair(band, d, q):
        here = 2 * d + band
        ry, cx, w00, w01, w10, w11 = (
            jnp.broadcast_to(T[here, i, pl.ds(q, 1), :], (16, 128)) for i in range(6)
        )
        first, second = sub == cx, sub == cx + 1.0
        upper = jnp.where(first, w00, jnp.where(second, w01, 0.0))
        lower = jnp.where(first, w10, jnp.where(second, w11, 0.0))
        levels = [
            jnp.where(ry == float(y), upper, jnp.where(ry == float(y - 1), lower, 0.0)).astype(BF)
            for y in range(16)
        ]
        matrix = jnp.concatenate(levels, axis=0).T
        near = F4[1 - d, pl.ds(band * 8, 16), pl.ds(pl.multiple_of(q * 16, 16), 32), :]
        blocks = []
        for k in range(2):
            window = near[:, 8 * k : 8 * k + 16].reshape(256, -1)
            made = jnp.dot(matrix[64 * k : 64 * k + 64], window, preferred_element_type=F32)
            blocks.append(made.reshape(8, 8, -1))
        Wp[d, pl.ds(1 + band * 8, 8), pl.ds(pl.multiple_of(EDGE + q * 16, 16), 16), :] = (
            jnp.concatenate(blocks, axis=1).astype(BF)
        )

    def warp(band):
        def two(i):
            for q in range(2):
                for d in range(2):
                    warp_pair(band, d, 2 * i + q)

        loop(width // 32, 0, two)

    def side(s, turn):
        return pltpu.make_async_remote_copy(
            src_ref=SO.at[turn, s - 2],
            dst_ref=SI.at[turn, s - 2],
            send_sem=side_send.at[s, turn],
            recv_sem=side_recv.at[s, turn],
            device_id=at(*DIRS[s]),
            device_id_type=MESH,
        )

    def side_pack(band, turn):
        for hand in range(2):
            lo, col = (EDGE, 0) if hand == 0 else (width, EDGE - 1)
            ends = [
                Wp[d, 1 + 8 * band + i, lo : lo + EDGE, :].astype(F32)[col : col + 1]
                for d in range(2) for i in range(8)
            ]
            SO[turn, hand] = jnp.concatenate(ends, axis=0).astype(BF)

    def side_column(d, row, hand, value):
        cols = pl.ds(EDGE + width, EDGE) if hand == 0 else pl.ds(0, EDGE)
        Wp[d, row, cols, :] = jnp.broadcast_to(value, (EDGE, feat)).astype(BF)

    def side_unpack(s, band, turn):
        side(s, turn).wait_recv()
        tile = SI[turn, s - 2].astype(F32)
        for d in range(2):
            for i in range(8):
                side_column(d, 1 + 8 * band + i, s - 2, tile[8 * d + i : 8 * d + i + 1])

    def border(s):
        dy, dx = DIRS[s]
        if dx == 0:
            src = Wp.at[:, rim(dy, 1, height, 1), pl.ds(EDGE, width)]
            dst = Wp.at[:, part(-dy, 1, height, 1), pl.ds(EDGE, width)]
        else:
            turn = 1 if n_ty == 2 or dy > 0 else 0
            src, dst = SO.at[turn, 0 if dx < 0 else 1], SC.at[s - 4]
        return pltpu.make_async_remote_copy(
            src_ref=src,
            dst_ref=dst,
            send_sem=rim_send.at[s],
            recv_sem=rim_recv.at[s],
            device_id=at(dy, dx),
            device_id_type=MESH,
        )

    def border_unpack(s):
        border(s).wait_recv()
        dy, dx = DIRS[s]
        if dx != 0:
            tile = SC[s - 4].astype(F32)
            for d in range(2):
                i = 8 * d + (0 if dy < 0 else 7)
                side_column(d, height + 1 if dy < 0 else 0, 0 if dx < 0 else 1, tile[i : i + 1])

    def each(sides, sign, act):
        for s in sides:
            dy, dx = DIRS[s]

            @pl.when(has(sign * dy, sign * dx))
            def _():
                act(s)

    across = (2, 3)
    along = (0, 1, 4, 5, 6, 7)
    everywhere = range(8)

    def coarse_warp():
        each(everywhere, -1, lambda s: list_copy(s).wait_recv())
        every = G[...].reshape(n * 2 * cells, -1)
        source = lax.broadcasted_iota(jnp.int32, (9 * 2 * cells, n * 2 * cells), 1).astype(F32)
        columns = LB[...].reshape(9 * 8, 128).T[:cells]
        warped = jnp.zeros((9 * 2 * cells, feat), F32)
        for e in range(2):
            at_lane = [8 * slot + 2 * d + e for slot in range(9) for d in range(2)]
            names = jnp.concatenate([columns[:, i : i + 1] for i in at_lane], axis=0)
            shares = jnp.concatenate([columns[:, i + 4 : i + 5] for i in at_lane], axis=0)
            chosen = jnp.where(source == names, shares, 0.0).astype(BF)
            warped = warped + jnp.dot(chosen, every, preferred_element_type=F32)
        CW[...] = warped.astype(BF).reshape(9, 2 * cells, feat)

    def coarse_flow():
        summed = jnp.zeros((2 * cells, feat), F32)
        for dy in (-1, 0, 1):
            own, other = {}, {}
            for dx in (-1, 0, 1):
                oy, ox = at(dy, dx)
                there = has(dy, dx)
                own[dx] = jnp.where(there, G[slot_of((oy, ox))].astype(F32), 0.0)
                slot = 8 if dy == 0 and dx == 0 else DIRS.index((-dy, -dx))
                other[dx] = CW[slot].astype(F32)
            columns = []
            for dx in (-1, 0, 1):
                for block in (own, other):
                    sides = []
                    for d in range(2):
                        lo = d * cells
                        mid = block[0][lo : lo + cells]
                        if dx < 0:
                            mid = jnp.concatenate([block[-1][lo + cells - 1 : lo + cells], mid[: cells - 1]], axis=0)
                        if dx > 0:
                            mid = jnp.concatenate([mid[1:], block[1][lo : lo + 1]], axis=0)
                        sides.append(mid)
                    columns.append(jnp.concatenate(sides, axis=0).astype(BF))
            summed = summed + jnp.dot(
                jnp.concatenate(columns, axis=1), W2[dy + 1, :, :feat], preferred_element_type=F32
            )
        hidden = jnp.maximum(summed + conv_b[...], 0.0).astype(BF)
        mixed = jnp.dot(hidden, mix2[:feat, :feat], preferred_element_type=F32) + mix_b[...]
        coarse = jnp.maximum(mixed, 0.0)
        ups = []
        for d in range(2):
            mine = coarse[d * cells : (d + 1) * cells]
            wide = jnp.broadcast_to(mine[:, None, :], (cells, POOL, feat)).reshape(width, -1)
            ups.append(nt(out_one, wide.astype(BF)))
        return ups

    conv_b2 = jnp.concatenate([conv_b[...]] * 2, axis=1)
    mix_b2 = jnp.concatenate([mix_b[...]] * 2, axis=1)

    def conv(start, pairs):
        def one(d):
            lhs = jnp.concatenate(
                [
                    jnp.concatenate([X[d, start + 2 * p + s] for p in range(pairs)], axis=0)
                    for s in range(4)
                ],
                axis=1,
            )
            summed = jnp.dot(lhs, W2[...].reshape(4 * 6 * feat, 2 * feat), preferred_element_type=F32)
            hidden = jnp.maximum(summed + conv_b2, 0.0).astype(BF)
            mixed = jnp.dot(hidden, mix2[...], preferred_element_type=F32) + mix_b2
            flow = nt(out_two, jnp.maximum(mixed, 0.0).astype(BF))
            for p in range(pairs):
                for j in range(2):
                    for k in range(2):
                        out[d, k, pl.ds(start + 2 * p + j, 1), :] = (
                            flow[2 * j + k : 2 * j + k + 1, p * width : (p + 1) * width] + out_b[k]
                        )

        loop(2, 0, one)

    if n_ty == 2:
        one = ty
        two = 1 - ty
        halo_wait(across)
        loop(height + MARGIN, MARGIN * one, shift)
        hand_on(1)
        warp(one)
        side_pack(one, 0)
        each(across, 1, lambda s: side(s, 0).start())
        loop(height + 1, one, functools.partial(spread, 0))
        each(across, -1, lambda s: side_unpack(s, one, 0))
        loop(9, 9 * one, functools.partial(spread, 1))
        hand_on(2)
        conv(10 * one, 3)
        hand_on(3)
        halo_wait(along)
        loop(MARGIN, (height + MARGIN) * two, shift)
        warp(two)
        side_pack(two, 1)
        each(across, 1, lambda s: side(s, 1).start())
        each(along, 1, lambda s: border(s).start())
        hand_on(4)
        spread(0, (height + 1) * two)
        each(across, -1, lambda s: side_unpack(s, two, 1))
        loop(8, 1 + 8 * two, functools.partial(spread, 1))
        conv(2 + 4 * two, 2)
        for j in range(5, len(steps) + 1):
            hand_on(j)
        coarse_warp()
        ups = coarse_flow()
        conv(6 + 4 * two, 2)
        each(along, -1, border_unpack)
        spread(1, (height + 1) * two)
        conv(14 * two, 1)
    else:
        one, two = 0, 1
        halo_wait(everywhere)
        loop(height + 2 * MARGIN, 0, shift)
        loop(height + 2, 0, functools.partial(spread, 0))
        warp(0)
        warp(1)
        side_pack(0, 0)
        each(across, 1, lambda s: side(s, 0).start())
        side_pack(1, 1)
        each(across, 1, lambda s: side(s, 1).start())
        each(along, 1, lambda s: border(s).start())
        for j in range(1, len(steps) + 1):
            hand_on(j)
        coarse_warp()
        ups = coarse_flow()
        each(along, -1, border_unpack)
        each(across, -1, lambda s: side_unpack(s, 0, 0))
        each(across, -1, lambda s: side_unpack(s, 1, 1))
        loop(height + 2, 0, functools.partial(spread, 1))
        conv(0, 4)
        conv(8, 4)

    for d in range(2):
        for k in range(2):
            out[d, k] = out[d, k] + (ups[d][k : k + 1] + out_b[k])

    each(everywhere, 1, lambda s: halo(s).wait_send())
    each(along, 1, lambda s: border(s).wait_send())
    each(across, 1, lambda s: side(s, 0).wait_send())
    each(across, 1, lambda s: side(s, 1).wait_send())
    each(everywhere, 1, lambda s: list_copy(s).wait_send())

    for j in range(len(steps)):
        hand(j).wait_send()


def on_device(
    n_ty, n_tx, frame_zero, frame_one, offset_whole, offset_frac, list_tile, list_pixel, list_weight,
    conv_weight, conv_bias, mix_weight, mix_bias, out_weight, out_bias,
):
    height, width, feat = frame_zero.shape
    cells = width // POOL
    n = n_ty * n_tx
    steps = max(n.bit_length() - 1, 1)
    vmem = pl.BlockSpec(memory_space=pltpu.VMEM)
    smem = pl.BlockSpec(memory_space=pltpu.SMEM)
    hbm = pl.BlockSpec(memory_space=pl.ANY)
    dma = pltpu.SemaphoreType.DMA
    return pl.pallas_call(
        functools.partial(kernel, n_ty, n_tx, height, width),
        out_shape=jax.ShapeDtypeStruct(offset_frac.shape, F32),
        in_specs=[hbm] * 4 + [smem] + [hbm] * 7 + [smem],
        out_specs=vmem,
        scratch_shapes=[
            pltpu.VMEM((2, height + 2 * MARGIN, width + 2 * EDGE, feat), BF),
            pltpu.VMEM((2, height + 2 * MARGIN, width + EDGE, feat), BF),
            pltpu.VMEM((2, height + 2, width + 2 * EDGE, feat), BF),
            pltpu.VMEM((2, height + 2, width, 6 * feat), BF),
            pltpu.VMEM((n, 2 * cells, feat), BF),
            pltpu.VMEM((9, 2 * cells, feat), BF),
            pltpu.VMEM((4, 6, 8, 128), F32),
            pltpu.VMEM((9, 8, 128), F32),
            pltpu.VMEM((2, 2, height * MARGIN, feat), BF),
            pltpu.VMEM((2, 2, height * MARGIN, feat), BF),
            pltpu.VMEM((4, 2, 16, feat), BF),
            pltpu.VMEM((2, 2, 16, feat), BF),
            pltpu.VMEM((2, 2, 16, feat), BF),
            pltpu.VMEM((4, 16, feat), BF),
            pltpu.VMEM(offset_whole.shape, jnp.int32),
            pltpu.VMEM(offset_frac.shape, F32),
            pltpu.VMEM(list_pixel.shape, jnp.int32),
            pltpu.VMEM((2, 1, 2, cells), BF),
            pltpu.VMEM((4, 6 * feat, 2 * feat), BF),
            pltpu.VMEM((2 * feat, 2 * feat), BF),
            pltpu.VMEM((1, feat), F32),
            pltpu.VMEM((1, feat), F32),
            pltpu.VMEM((2, feat), BF),
            dma((13,)), dma((8,)), dma((8,)), dma((steps,)), dma((steps,)),
            dma((8,)), dma((8,)), dma((8, 2)), dma((8, 2)), dma((8,)), dma((8,)),
        ],
        compiler_params=pltpu.CompilerParams(
            collective_id=0, has_side_effects=True, vmem_limit_bytes=60 * 2**20
        ),
    )(
        frame_zero, frame_one, offset_whole, offset_frac, list_tile.transpose(0, 2, 3, 1), list_pixel,
        list_weight.transpose(0, 2, 1, 3), conv_weight.reshape(3, 6 * feat, feat), conv_bias.reshape(1, -1), mix_weight,
        mix_bias.reshape(1, -1), out_weight.T, out_bias,
    )


def solution(mesh):
    tiles = P(None, None, "ty", "tx")
    in_specs = (P("ty", "tx", None),) * 2 + (tiles,) * 5 + (P(),) * 6
    run = functools.partial(on_device, mesh.shape["ty"], mesh.shape["tx"])
    return jax.shard_map(run, mesh=mesh, in_specs=in_specs, out_specs=tiles, check_vma=False)
```
